512 devices in a mesh: dp: 32 (over z_hi, x, y), ctx: 16 (over z_lo, core).
Axes of the slice: x: 4, y: 4, z: 16 (z_hi: 2, z_lo: 8; z = z_hi * 8 + z_lo), core: 2. Of those that a mesh axis runs over, the one named last changes fastest.
Arguments:
- query_rows: bfloat16 [32, 1024, 4096], P('dp', 'ctx'), may hold values from -40 to 40
- key_rows: bfloat16 [32, 1024, 4096], P('dp', 'ctx'), may hold values from -40 to 40
- value_rows: bfloat16 [32, 1024, 4096], P('dp', 'ctx'), may hold values from -6 to 6
- query_tangent: bfloat16 [32, 1024, 4096], P('dp', 'ctx'), may hold values from -6 to 6
- key_tangent: bfloat16 [32, 1024, 4096], P('dp', 'ctx'), may hold values from -6 to 6
- value_tangent: bfloat16 [32, 1024, 4096], P('dp', 'ctx'), may hold values from -6 to 6
- query_gain: bfloat16 [4096], P('dp'), may hold values from 1.1953125 to 2.390625
- key_gain: bfloat16 [4096], P('dp'), may hold values from 1.1953125 to 2.390625
Outputs:
- attended: bfloat16 [32, 1024, 4096], P('dp', 'ctx')
- attended_tangent: bfloat16 [32, 1024, 4096], P('dp', 'ctx')
The draws below stay inside these ranges and needn't reach their ends.
All inputs are finite; a program needn't handle non-finite values.
Results may differ from the reference program's by a relative error of at most 0.0065.
The reference program's roundings to bfloat16 on the way count: a program that leaves them out, or rounds other values in their place, can miss the bound.
Values may be sent and summed in bfloat16 or wider, within the bound.
No kernel may reach another device: no remote copies, remote signals or barrier semaphores. Data moves between devices by JAX's collectives and lax.ppermute only.
A program may use at most 64 MiB of HBM per device.

```python
import math
import jax
import jax.numpy as jnp
from jax import lax

HEADS = 32
HEAD_DIM = 128
WIDTH = 4096
SEQ = 1024
SAMPLES = 32


def draw_query_rows(key, part):
    key = jax.random.fold_in(key, 1)
    values = jnp.clip(jax.random.normal(key, (SAMPLES, SEQ, WIDTH), jnp.float32), -4.0, 4.0)
    return values.astype(jnp.bfloat16)


def draw_key_rows(key, part):
    key = jax.random.fold_in(key, 2)
    values = jnp.clip(jax.random.normal(key, (SAMPLES, SEQ, WIDTH), jnp.float32), -4.0, 4.0)
    return values.astype(jnp.bfloat16)


def level_of(stream_key, shape, pieces, smallest, top_value):
    def one(dim, blocks):
        steps = jax.random.uniform(jax.random.fold_in(jax.random.fold_in(stream_key, 6), dim), (blocks,), jnp.float32, smallest / len(pieces), top_value / len(pieces))
        return jnp.repeat(jnp.exp(steps), shape[dim] // blocks).reshape((-1,) + (1,) * (len(shape) - dim - 1))

    gain = one(*pieces[0])
    for cut in pieces[1:]:
        gain = gain * one(*cut)
    return gain


def normal_values(rng, extent, spread, reach, cuts=(), dtype=jnp.bfloat16):
    values = spread * jax.random.normal(rng, extent, jnp.float32)
    if cuts:
        values = values * level_of(rng, extent, cuts, -0.22, 0.18)
    return jnp.clip(values, -reach, reach).astype(dtype)


def setup_inputs(seed: int = 0) -> dict:
    splits = jax.random.split(jax.random.key(seed), 9)
    query_rows = draw_query_rows(jax.random.fold_in(splits[8], 71), 0)
    key_rows = draw_key_rows(jax.random.fold_in(splits[8], 71), 0)
    value_rows = normal_values(splits[2], (SAMPLES, SEQ, WIDTH), 1.0, 6.0, ((0, 32), (1, 16)))
    query_tangent = normal_values(splits[3], (SAMPLES, SEQ, WIDTH), 1.0, 6.0, ((0, 32), (1, 16)))
    key_tangent = normal_values(splits[4], (SAMPLES, SEQ, WIDTH), 1.0, 6.0, ((0, 32), (1, 16)))
    value_tangent = normal_values(splits[5], (SAMPLES, SEQ, WIDTH), 1.0, 6.0, ((0, 32), (1, 16)))
    query_gain = jnp.clip(jnp.exp(math.log(2.390625) - 0.6931472 * jax.random.uniform(splits[6], (WIDTH,), jnp.float32) ** level_of(splits[6], (WIDTH,), ((0, 32),), -0.2, 0.2)), 1.1953125, 2.390625).astype(jnp.bfloat16)
    key_gain = jnp.clip(jnp.exp(math.log(2.390625) - 0.6931472 * jax.random.uniform(splits[7], (WIDTH,), jnp.float32) ** level_of(splits[7], (WIDTH,), ((0, 32),), -0.2, 0.2)), 1.1953125, 2.390625).astype(jnp.bfloat16)
    return dict(query_rows=query_rows, key_rows=key_rows, value_rows=value_rows, query_tangent=query_tangent, key_tangent=key_tangent, value_tangent=value_tangent, query_gain=query_gain, key_gain=key_gain)


CONTRACT = (((1,), (1,)), ((), ()))

def normalize(rows_in, tangent_in, gain_full):
    values = rows_in.astype(jnp.float32)
    tangent = tangent_in.astype(jnp.float32)
    gain_f = gain_full.astype(jnp.float32)
    inverse = lax.rsqrt(lax.optimization_barrier(jnp.mean(values * values, axis=-1, keepdims=True)) + 1e-06)
    cross = lax.optimization_barrier(jnp.mean(values * tangent, axis=-1, keepdims=True))
    normed = (values * inverse * gain_f).astype(jnp.bfloat16)
    normed_tangent = ((tangent * inverse - values * (inverse * inverse * inverse) * cross) * gain_f).astype(jnp.bfloat16)
    return (normed, normed_tangent)

def single_head(operands):
    queries, queries_dot, keys_in, keys_dot, values, values_dot = operands
    factor = queries.shape[-1] ** (-0.5)
    scores = lax.dot_general(queries, keys_in, CONTRACT, preferred_element_type=jnp.float32) * factor
    scores_dot = (lax.dot_general(queries_dot, keys_in, CONTRACT, preferred_element_type=jnp.float32) + lax.dot_general(queries, keys_dot, CONTRACT, preferred_element_type=jnp.float32)) * factor
    peak = lax.optimization_barrier(jnp.max(scores, axis=-1, keepdims=True))
    exponent = jnp.exp(scores - peak)
    weights = exponent / lax.optimization_barrier(jnp.sum(exponent, axis=-1, keepdims=True))
    weights_dot = weights * (scores_dot - lax.optimization_barrier(jnp.sum(weights * scores_dot, axis=-1, keepdims=True)))
    probs = weights.astype(jnp.bfloat16)
    probs_dot = weights_dot.astype(jnp.bfloat16)
    output = jnp.dot(probs, values, preferred_element_type=jnp.float32)
    output_dot = jnp.dot(probs_dot, values, preferred_element_type=jnp.float32) + jnp.dot(probs, values_dot, preferred_element_type=jnp.float32)
    return (output.astype(jnp.bfloat16), output_dot.astype(jnp.bfloat16))

def reference(query_rows, key_rows, value_rows, query_tangent, key_tangent, value_tangent, query_gain, key_gain):

    def per_sample(items):
        q_in, qd_in, k_in, kd_in, v_in, vd_in = items
        query_normed, query_dot = normalize(q_in, qd_in, query_gain)
        key_normed, key_dot = normalize(k_in, kd_in, key_gain)

        def to_heads(array):
            return jnp.moveaxis(array.reshape(SEQ, HEADS, HEAD_DIM), 1, 0)
        output, output_dot = lax.map(single_head, (to_heads(query_normed), to_heads(query_dot), to_heads(key_normed), to_heads(key_dot), to_heads(v_in), to_heads(vd_in)))
        return (jnp.moveaxis(output, 0, 1).reshape(SEQ, WIDTH), jnp.moveaxis(output_dot, 0, 1).reshape(SEQ, WIDTH))
    attended, attended_tangent = lax.map(per_sample, (query_rows, query_tangent, key_rows, key_tangent, value_rows, value_tangent))
    return (attended, attended_tangent)
```

```python
import jax
import jax.numpy as jnp
from jax import lax
from jax.experimental import pallas as pl
from jax.experimental.pallas import tpu as pltpu
from jax.sharding import PartitionSpec as P

HEAD_DIM = 128
CHIPS = 8
HEADS_PER_CHIP = 4
TOKENS = 64
FEATURES = HEADS_PER_CHIP * HEAD_DIM
STAT_ROWS = 16
ARRAYS = 6
ROWS = ARRAYS * HEADS_PER_CHIP * TOKENS + STAT_ROWS
LOG2E = 1.4426950408889634
VMEM = 56 * 1024 * 1024


def vmem_spec():
    return pl.BlockSpec(memory_space=pltpu.VMEM)


def smem_spec():
    return pl.BlockSpec(memory_space=pltpu.SMEM)


def params():
    return pltpu.CompilerParams(vmem_limit_bytes=VMEM)


def pack_kernel(chip_ref, *refs):
    ins, outs = refs[:ARRAYS], refs[ARRAYS:]
    chip = chip_ref[0]
    columns = []
    for values_ref, tangent_ref in ((ins[0], ins[1]), (ins[2], ins[3])):
        square = jnp.zeros((TOKENS, HEAD_DIM), jnp.float32)
        cross = jnp.zeros((TOKENS, HEAD_DIM), jnp.float32)
        width = values_ref.shape[1]
        for start in range(0, width, HEAD_DIM):
            values = values_ref[:, start : start + HEAD_DIM].astype(jnp.float32)
            tangent = tangent_ref[:, start : start + HEAD_DIM].astype(jnp.float32)
            square += values * values
            cross += values * tangent
        mean_square = jnp.sum(square, axis=1, keepdims=True) / width
        columns.append(lax.rsqrt(mean_square + 1e-06))
        columns.append(jnp.sum(cross, axis=1, keepdims=True) / width)
    lane = lax.broadcasted_iota(jnp.int32, (TOKENS, HEAD_DIM), 1)
    table = jnp.zeros((TOKENS, HEAD_DIM), jnp.float32)
    for index, column in enumerate(columns):
        rest = column
        for part in range(3):
            piece = rest.astype(jnp.bfloat16).astype(jnp.float32)
            rest = rest - piece
            table = jnp.where(lane == part * 4 + index, piece, table)
    table = jnp.concatenate([table, jnp.zeros((HEAD_DIM - TOKENS, HEAD_DIM), jnp.float32)], axis=0)
    stats = jnp.transpose(table)[:STAT_ROWS].astype(jnp.bfloat16)
    for step in range(CHIPS):
        target = jnp.bitwise_xor(chip, step)
        for array in range(ARRAYS):
            for head in range(HEADS_PER_CHIP):
                row = (array * HEADS_PER_CHIP + head) * TOKENS
                column = pl.multiple_of(target * FEATURES + head * HEAD_DIM, HEAD_DIM)
                outs[step][row : row + TOKENS, :] = ins[array][:, pl.ds(column, HEAD_DIM)]
        outs[step][ROWS - STAT_ROWS : ROWS, :] = stats


def norm_kernel(gain_ref, *refs):
    blocks, (query_ref, kv_ref) = refs[:CHIPS], refs[CHIPS:]
    for step in range(CHIPS):
        block = blocks[step]
        parts = block[ROWS - STAT_ROWS : ROWS, :].astype(jnp.float32)
        rows = parts[0:4] + (parts[4:8] + parts[8:12])
        rows = jnp.concatenate([rows, jnp.zeros((HEAD_DIM - 4, HEAD_DIM), jnp.float32)], axis=0)
        columns = jnp.transpose(rows)[:TOKENS]
        where = pl.ds(step * TOKENS, TOKENS)

        def rows_of(array, head, block=block):
            row = (array * HEADS_PER_CHIP + head) * TOKENS
            return block[row : row + TOKENS, :]

        for norm, target in ((0, query_ref), (1, kv_ref)):
            inverse = columns[:, 2 * norm : 2 * norm + 1]
            cross = columns[:, 2 * norm + 1 : 2 * norm + 2]
            cube = inverse * inverse * inverse
            for head in range(HEADS_PER_CHIP):
                gain = gain_ref[norm, head : head + 1, :].astype(jnp.float32)
                values = rows_of(2 * norm, head).astype(jnp.float32)
                tangent = rows_of(2 * norm + 1, head).astype(jnp.float32)
                normed = values * inverse * gain
                normed_tangent = (tangent * inverse - values * cube * cross) * gain
                target[0, head, where, :] = normed.astype(jnp.bfloat16)
                target[1, head, where, :] = normed_tangent.astype(jnp.bfloat16)
        for head in range(HEADS_PER_CHIP):
            kv_ref[2, head, where, :] = rows_of(4, head)
            kv_ref[3, head, where, :] = rows_of(5, head)


QUERY_BLOCK = 256
CONTRACT = (((1,), (1,)), ((), ()))


def attend_kernel(query_ref, own_ref, other_ref, *outs):
    factor = HEAD_DIM**-0.5

    def head_step(head, carry):
        def both(index):
            return jnp.concatenate([own_ref[index, head], other_ref[index, head]], axis=0)

        keys, keys_dot, values, values_dot = both(0), both(1), both(2), both(3)
        keys_pair = jnp.concatenate([keys, keys_dot], axis=1)
        values_pair = jnp.concatenate([values, values_dot], axis=1)
        total = query_ref.shape[2]
        for start in range(0, total, QUERY_BLOCK):
            queries = query_ref[0, head, start : start + QUERY_BLOCK, :]
            queries_dot = query_ref[1, head, start : start + QUERY_BLOCK, :]
            queries_pair = jnp.concatenate([queries_dot, queries], axis=1)
            scores = lax.dot_general(queries, keys, CONTRACT, preferred_element_type=jnp.float32)
            scores_dot = lax.dot_general(
                queries_pair, keys_pair, CONTRACT, preferred_element_type=jnp.float32
            )
            peak = jnp.max(scores, axis=1, keepdims=True)
            exponent = jnp.exp2((scores - peak) * (factor * LOG2E))
            scale = 1.0 / jnp.sum(exponent, axis=1, keepdims=True)
            weights = exponent * scale
            mean = jnp.sum(weights * scores_dot, axis=1, keepdims=True)
            weights_dot = (weights * factor) * (scores_dot - mean)
            probs = weights.astype(jnp.bfloat16)
            probs_dot = weights_dot.astype(jnp.bfloat16)
            pair = jnp.dot(probs, values_pair, preferred_element_type=jnp.float32)
            output_dot = jnp.dot(probs_dot, values, preferred_element_type=jnp.float32)
            output = pair[:, :HEAD_DIM].astype(jnp.bfloat16)
            output_dot = (output_dot + pair[:, HEAD_DIM:]).astype(jnp.bfloat16)
            for piece in range(QUERY_BLOCK // TOKENS):
                out = outs[start // TOKENS + piece]
                row = pl.multiple_of(head * TOKENS, TOKENS)
                rows = slice(piece * TOKENS, (piece + 1) * TOKENS)
                out[0, pl.ds(row, TOKENS), :] = output[rows]
                out[1, pl.ds(row, TOKENS), :] = output_dot[rows]
        return carry

    lax.fori_loop(0, HEADS_PER_CHIP, head_step, 0)


def unpack_kernel(chip_ref, *refs):
    blocks, outs = refs[:CHIPS], refs[CHIPS:]
    chip = chip_ref[0]
    for step in range(CHIPS):
        source = jnp.bitwise_xor(chip, step)
        for index in range(2):
            for head in range(HEADS_PER_CHIP):
                column = pl.multiple_of(source * FEATURES + head * HEAD_DIM, HEAD_DIM)
                rows = slice(head * TOKENS, (head + 1) * TOKENS)
                outs[index][:, pl.ds(column, HEAD_DIM)] = blocks[step][index, rows, :]


def exchange(block, step):
    pairs = [(place, place ^ (2 * step)) for place in range(2 * CHIPS)]
    return lax.ppermute(block, "ctx", pairs)


def swap(block):
    return lax.ppermute(block, "ctx", [(place, place ^ 1) for place in range(2 * CHIPS)])


def local(
    query_rows,
    key_rows,
    value_rows,
    query_tangent,
    key_tangent,
    value_tangent,
    query_gain,
    key_gain,
):
    rows, width = query_rows.shape[1:]
    chip = (lax.axis_index("ctx") // 2).astype(jnp.int32)
    chip_ref = chip.reshape(1)

    shards = lax.axis_size("dp")
    gains = jnp.stack([query_gain, key_gain])
    gains = jnp.broadcast_to(gains[None], (shards, *gains.shape))
    gains = lax.all_to_all(gains, "dp", 0, 0, tiled=True)
    gains = jnp.moveaxis(gains, 0, 1).reshape(2, width // HEAD_DIM, HEAD_DIM)
    gains = lax.dynamic_slice_in_dim(gains, chip * HEADS_PER_CHIP, HEADS_PER_CHIP, axis=1)

    blocks = pl.pallas_call(
        pack_kernel,
        out_shape=[jax.ShapeDtypeStruct((ROWS, HEAD_DIM), jnp.bfloat16)] * CHIPS,
        in_specs=[smem_spec()] + [vmem_spec()] * ARRAYS,
        out_specs=[vmem_spec()] * CHIPS,
        compiler_params=params(),
        name="pack",
    )(
        chip_ref,
        query_rows[0],
        query_tangent[0],
        key_rows[0],
        key_tangent[0],
        value_rows[0],
        value_tangent[0],
    )
    arrived = [blocks[0]] + [exchange(blocks[step], step) for step in range(1, CHIPS)]

    many = CHIPS * TOKENS
    queries, own = pl.pallas_call(
        norm_kernel,
        out_shape=[
            jax.ShapeDtypeStruct((2, HEADS_PER_CHIP, many, HEAD_DIM), jnp.bfloat16),
            jax.ShapeDtypeStruct((4, HEADS_PER_CHIP, many, HEAD_DIM), jnp.bfloat16),
        ],
        in_specs=[vmem_spec()] * (1 + CHIPS),
        out_specs=[vmem_spec()] * 2,
        compiler_params=params(),
        name="norm",
    )(gains, *arrived)
    other = swap(own)

    outs = pl.pallas_call(
        attend_kernel,
        out_shape=[
            jax.ShapeDtypeStruct((2, HEADS_PER_CHIP * TOKENS, HEAD_DIM), jnp.bfloat16)
        ] * CHIPS,
        in_specs=[vmem_spec()] * 3,
        out_specs=[vmem_spec()] * CHIPS,
        compiler_params=params(),
        name="attend",
    )(queries, own, other)
    back = [outs[0]] + [exchange(outs[step], step) for step in range(1, CHIPS)]

    attended, attended_tangent = pl.pallas_call(
        unpack_kernel,
        out_shape=[jax.ShapeDtypeStruct((rows, width), jnp.bfloat16)] * 2,
        in_specs=[smem_spec()] + [vmem_spec()] * CHIPS,
        out_specs=[vmem_spec()] * 2,
        compiler_params=params(),
        name="unpack",
    )(chip_ref, *back)
    return attended[None], attended_tangent[None]


def solution(mesh):
    rows = P("dp", "ctx", None)
    return jax.shard_map(
        local,
        mesh=mesh,
        in_specs=(rows,) * 6 + (P("dp"), P("dp")),
        out_specs=(rows, rows),
        check_vma=False,
    )
```

```python
import functools

import jax
import jax.numpy as jnp
from jax import lax
from jax.experimental import pallas as pl
from jax.experimental.pallas import tpu as pltpu
from jax.sharding import PartitionSpec as P

HEAD_DIM = 128
CHIPS = 8
HEADS_PER_CHIP = 4
TOKENS = 64
FEATURES = HEADS_PER_CHIP * HEAD_DIM
BLOCK = HEADS_PER_CHIP * TOKENS
STAT_ROWS = 16
ARRAYS = 6
STEPS = (4, 1, 5, 2, 3, 6, 7, 0)
LATE = (5, 6)
EARLY = (0, 1, 2, 3, 4, 7)
ORDER = (0, 2, 5, 6, 1, 3, 4, 7)
PACK_MIB = 56
LOG2E = 1.4426950408889634
MIB = 1024 * 1024


def vmem(count):
    return [pl.BlockSpec(memory_space=pltpu.VMEM)] * count


def smem():
    return [pl.BlockSpec(memory_space=pltpu.SMEM)]


def params(mib):
    return pltpu.CompilerParams(vmem_limit_bytes=mib * MIB)


def shape(*sizes, dtype=jnp.bfloat16):
    return jax.ShapeDtypeStruct(sizes, dtype)


def statistics(pairs):
    columns = []
    for values_ref, tangent_ref in pairs:
        square = jnp.zeros((TOKENS, HEAD_DIM), jnp.float32)
        cross = jnp.zeros((TOKENS, HEAD_DIM), jnp.float32)
        width = values_ref.shape[1]
        for start in range(0, width, HEAD_DIM):
            values = values_ref[:, start : start + HEAD_DIM].astype(jnp.float32)
            tangent = tangent_ref[:, start : start + HEAD_DIM].astype(jnp.float32)
            square += values * values
            cross += values * tangent
        mean_square = jnp.sum(square, axis=1, keepdims=True) / width
        columns.append(lax.rsqrt(mean_square + 1e-06))
        columns.append(jnp.sum(cross, axis=1, keepdims=True) / width)
    lane = lax.broadcasted_iota(jnp.int32, (TOKENS, HEAD_DIM), 1)
    table = jnp.zeros((TOKENS, HEAD_DIM), jnp.float32)
    for index, column in enumerate(columns):
        rest = column
        for part in range(3):
            piece = rest.astype(jnp.bfloat16).astype(jnp.float32)
            rest = rest - piece
            table = jnp.where(lane == part * 4 + index, piece, table)
    table = jnp.concatenate([table, jnp.zeros((HEAD_DIM - TOKENS, HEAD_DIM), jnp.float32)], axis=0)
    return jnp.transpose(table)[:STAT_ROWS].astype(jnp.bfloat16)


def table_of(stats):
    parts = stats.astype(jnp.float32)
    rows = parts[0:4] + (parts[4:8] + parts[8:12])
    rows = jnp.concatenate([rows, jnp.zeros((HEAD_DIM - 4, HEAD_DIM), jnp.float32)], axis=0)
    return jnp.transpose(rows)[:TOKENS]


def normed(values, tangent, columns, which, gain):
    inverse = columns[:, 2 * which : 2 * which + 1]
    cross = columns[:, 2 * which + 1 : 2 * which + 2]
    cube = inverse * inverse * inverse
    values = values.astype(jnp.float32)
    tangent = tangent.astype(jnp.float32)
    gain = gain.astype(jnp.float32)
    rows = (values * inverse * gain).astype(jnp.bfloat16)
    return rows, ((tangent * inverse - values * cube * cross) * gain).astype(jnp.bfloat16)


def copy_columns(chip, arrays, out, place):
    target = jnp.bitwise_xor(chip, STEPS[place])
    for index, array in enumerate(arrays):
        for head in range(HEADS_PER_CHIP):
            column = pl.multiple_of(target * FEATURES + head * HEAD_DIM, HEAD_DIM)
            row = index * BLOCK + head * TOKENS
            out[row : row + TOKENS, :] = array[:, pl.ds(column, HEAD_DIM)]


def pack_kernel(chip_ref, *refs):
    arrays, outs, late = refs[:ARRAYS], refs[ARRAYS : ARRAYS + CHIPS], refs[ARRAYS + CHIPS :]
    stats = statistics((arrays[4:], arrays[:2]))
    for place, out in enumerate(outs):
        kept = arrays[:4] if place in LATE else arrays
        copy_columns(chip_ref[0], kept, out, place)
        out[len(kept) * BLOCK :, :] = stats
    for place, out in zip(LATE, late):
        copy_columns(chip_ref[0], arrays[4:], out, place)


def norm_kernel(gain_ref, *refs):
    blocks, (kv_ref, table_ref) = refs[:CHIPS], refs[CHIPS:]
    for place, block in enumerate(blocks):
        where = pl.ds(place * TOKENS, TOKENS)
        columns = table_of(block[block.shape[0] - STAT_ROWS :, :])
        table_ref[where, :] = columns
        for head in range(HEADS_PER_CHIP):
            rows = [block[i * BLOCK + head * TOKENS :][:TOKENS] for i in range(4)]
            rows[:2] = normed(rows[0], rows[1], columns, 1, gain_ref[1, head : head + 1, :])
            for index in range(4):
                kv_ref[index, head, where, :] = rows[index]


CONTRACT = (((1,), (1,)), ((), ()))


def attend_kernel(places, gain_ref, table_ref, own_ref, other_ref, *refs):
    blocks, outs = refs[: len(places)], refs[len(places) :]
    factor = HEAD_DIM**-0.5
    for head in range(HEADS_PER_CHIP):

        def both(index, head=head):
            return jnp.concatenate([own_ref[index, head], other_ref[index, head]], axis=0)

        keys, keys_dot, values, values_dot = both(0), both(1), both(2), both(3)
        keys_pair = jnp.concatenate([keys, keys_dot], axis=1)
        values_pair = jnp.concatenate([values, values_dot], axis=1)
        token = slice(head * TOKENS, (head + 1) * TOKENS)
        tangent_token = slice(BLOCK + head * TOKENS, BLOCK + (head + 1) * TOKENS)
        pairs = []
        for place, block in zip(places, blocks):
            first = block.shape[0] - 2 * BLOCK if place in LATE else 4 * BLOCK
            rows = [block[first + i * BLOCK + head * TOKENS :][:TOKENS] for i in range(2)]
            columns = table_ref[place * TOKENS : (place + 1) * TOKENS, :]
            pairs.append(normed(*rows, columns, 0, gain_ref[0, head : head + 1, :]))
        queries = jnp.concatenate([pair[0] for pair in pairs], axis=0)
        queries_dot = jnp.concatenate([pair[1] for pair in pairs], axis=0)
        queries_pair = jnp.concatenate([queries_dot, queries], axis=1)
        scores = lax.dot_general(queries, keys, CONTRACT, preferred_element_type=jnp.float32)
        scores_dot = lax.dot_general(
            queries_pair, keys_pair, CONTRACT, preferred_element_type=jnp.float32
        )
        peak = jnp.max(scores, axis=1, keepdims=True)
        exponent = jnp.exp2((scores - peak) * (factor * LOG2E))
        scale = 1.0 / jnp.sum(exponent, axis=1, keepdims=True)
        weights = exponent * scale
        mean = jnp.sum(weights * scores_dot, axis=1, keepdims=True)
        weights_dot = (weights * factor) * (scores_dot - mean)
        probs = weights.astype(jnp.bfloat16)
        probs_dot = weights_dot.astype(jnp.bfloat16)
        pair = jnp.dot(probs, values_pair, preferred_element_type=jnp.float32)
        output_dot = jnp.dot(probs_dot, values, preferred_element_type=jnp.float32)
        output = pair[:, :HEAD_DIM].astype(jnp.bfloat16)
        output_dot = (output_dot + pair[:, HEAD_DIM:]).astype(jnp.bfloat16)
        for index, out in enumerate(outs):
            rows = slice(index * TOKENS, (index + 1) * TOKENS)
            out[token, :] = output[rows]
            out[tangent_token, :] = output_dot[rows]


def unpack_kernel(chip_ref, *refs):
    blocks, outs = refs[:CHIPS], refs[CHIPS:]
    for block, place in zip(blocks, ORDER):
        source = jnp.bitwise_xor(chip_ref[0], STEPS[place])
        for index, out in enumerate(outs):
            for head in range(HEADS_PER_CHIP):
                column = pl.multiple_of(source * FEATURES + head * HEAD_DIM, HEAD_DIM)
                row = index * BLOCK + head * TOKENS
                out[:, pl.ds(column, HEAD_DIM)] = block[row : row + TOKENS, :]


def exchange(block, step):
    pairs = [(place, place ^ (2 * step)) for place in range(2 * CHIPS)]
    return lax.ppermute(block, "ctx", pairs)


def swap(block):
    return lax.ppermute(block, "ctx", [(place, place ^ 1) for place in range(2 * CHIPS)])


def after(block, other):
    return lax.optimization_barrier((block, other))


def send(blocks, places=range(CHIPS)):
    steps = [STEPS[place] for place in places]
    return [exchange(block, step) if step else block for block, step in zip(blocks, steps)]


def gather_gains(gains, chip):
    shards = lax.axis_size("dp")
    gains = gains.reshape(2, -1, HEAD_DIM)
    place = lax.axis_index("dp")

    def partner(array, bit):
        return lax.ppermute(array, "dp", [(one, one ^ bit) for one in range(shards)])

    bit = 1
    while gains.shape[1] < HEADS_PER_CHIP:
        other = partner(gains, bit)
        mine_first = jnp.concatenate([gains, other], axis=1)
        mine_last = jnp.concatenate([other, gains], axis=1)
        gains = jnp.where(place & bit == 0, mine_first, mine_last)
        bit *= 2
    if gains.shape[1] > HEADS_PER_CHIP:
        return lax.dynamic_slice_in_dim(gains, chip * HEADS_PER_CHIP, HEADS_PER_CHIP, axis=1)
    wanted = chip * bit
    while bit < shards:
        gains = jnp.where((place ^ wanted) & bit == 0, gains, partner(gains, bit))
        bit *= 2
    return gains


def local(q, k, v, qd, kd, vd, query_gain, key_gain):
    q, k, v, qd, kd, vd = (array[0] for array in (q, k, v, qd, kd, vd))
    chip = (lax.axis_index("ctx") // 2).astype(jnp.int32)
    chip_ref = chip.reshape(1)

    sizes = [4 if place in LATE else ARRAYS for place in range(CHIPS)]
    blocks = pl.pallas_call(
        pack_kernel,
        out_shape=[shape(size * BLOCK + STAT_ROWS, HEAD_DIM) for size in sizes]
        + [shape(2 * BLOCK, HEAD_DIM)] * len(LATE),
        in_specs=smem() + vmem(ARRAYS),
        out_specs=vmem(CHIPS + len(LATE)),
        compiler_params=params(PACK_MIB),
        name="pack",
    )(chip_ref, k, kd, v, vd, q, qd)
    blocks, late = blocks[:CHIPS], blocks[CHIPS:]
    arrived = send(blocks[:5])
    for place, gate in zip(LATE, (1, 3)):
        block, arrived[gate] = after(blocks[place], arrived[gate])
        arrived.append(exchange(block, STEPS[place]))
    arrived.append(blocks[7])
    late = [exchange(block, STEPS[place]) for block, place in zip(late, LATE)]

    gains = jnp.stack([query_gain, key_gain])
    gains, arrived[2] = after(gains, arrived[2])
    gains = gather_gains(gains, chip)

    many = CHIPS * TOKENS
    own, table = pl.pallas_call(
        norm_kernel,
        out_shape=[
            shape(4, HEADS_PER_CHIP, many, HEAD_DIM),
            shape(many, HEAD_DIM, dtype=jnp.float32),
        ],
        in_specs=vmem(1 + CHIPS),
        out_specs=vmem(2),
        compiler_params=params(16),
        name="norm",
    )(gains, *arrived)
    other = swap(own)

    def attend(places, blocks):
        return pl.pallas_call(
            functools.partial(attend_kernel, places),
            out_shape=[shape(2 * BLOCK, HEAD_DIM)] * len(places),
            in_specs=vmem(4 + len(places)),
            out_specs=vmem(len(places)),
            compiler_params=params(32),
            name="attend",
        )(gains, table, own, other, *blocks)

    outs = dict(zip(EARLY, attend(EARLY, [arrived[place] for place in EARLY])))
    outs.update(zip(LATE, attend(LATE, late)))
    back = dict(zip(ORDER, send([outs[place] for place in ORDER], ORDER)))

    rows, width = q.shape
    attended, attended_tangent = pl.pallas_call(
        unpack_kernel,
        out_shape=[shape(rows, width)] * 2,
        in_specs=smem() + vmem(CHIPS),
        out_specs=vmem(2),
        compiler_params=params(16),
        name="unpack",
    )(chip_ref, *[back[place] for place in ORDER])
    return attended[None], attended_tangent[None]


def solution(mesh):
    rows = P("dp", "ctx", None)
    return jax.shard_map(
        local,
        mesh=mesh,
        in_specs=(rows,) * 6 + (P("dp"), P("dp")),
        out_specs=(rows, rows),
        check_vma=False,
    )
```

```python
import functools

import jax
import jax.numpy as jnp
from jax import lax
from jax.experimental import pallas as pl
from jax.experimental.pallas import tpu as pltpu
from jax.sharding import PartitionSpec as P

HEAD_DIM = 128
CHIPS = 8
HEADS_PER_CHIP = 4
TOKENS = 64
FEATURES = HEADS_PER_CHIP * HEAD_DIM
BLOCK = HEADS_PER_CHIP * TOKENS
STAT_ROWS = 16
ARRAYS = 6
STEPS = (4, 1, 5, 2, 3, 6, 7, 0)
LATE = (5, 6)
EARLY = (0, 1, 2, 3, 4, 7)
ORDER = (0, 2, 5, 6, 1, 3, 4, 7)
PACK_MIB = 56
LOG2E = 1.4426950408889634
MIB = 1024 * 1024


def vmem(count):
    return [pl.BlockSpec(memory_space=pltpu.VMEM)] * count


def smem():
    return [pl.BlockSpec(memory_space=pltpu.SMEM)]


def params(mib):
    return pltpu.CompilerParams(vmem_limit_bytes=mib * MIB)


def shape(*sizes, dtype=jnp.bfloat16):
    return jax.ShapeDtypeStruct(sizes, dtype)


def statistics(pairs):
    columns = []
    for values_ref, tangent_ref in pairs:
        square = jnp.zeros((TOKENS, HEAD_DIM), jnp.float32)
        cross = jnp.zeros((TOKENS, HEAD_DIM), jnp.float32)
        width = values_ref.shape[1]
        for start in range(0, width, HEAD_DIM):
            values = values_ref[:, start : start + HEAD_DIM].astype(jnp.float32)
            tangent = tangent_ref[:, start : start + HEAD_DIM].astype(jnp.float32)
            square += values * values
            cross += values * tangent
        mean_square = jnp.sum(square, axis=1, keepdims=True) / width
        columns.append(lax.rsqrt(mean_square + 1e-06))
        columns.append(jnp.sum(cross, axis=1, keepdims=True) / width)
    lane = lax.broadcasted_iota(jnp.int32, (TOKENS, HEAD_DIM), 1)
    table = jnp.zeros((TOKENS, HEAD_DIM), jnp.float32)
    for index, column in enumerate(columns):
        rest = column
        for part in range(3):
            piece = rest.astype(jnp.bfloat16).astype(jnp.float32)
            rest = rest - piece
            table = jnp.where(lane == part * 4 + index, piece, table)
    table = jnp.concatenate([table, jnp.zeros((HEAD_DIM - TOKENS, HEAD_DIM), jnp.float32)], axis=0)
    return jnp.transpose(table)[:STAT_ROWS].astype(jnp.bfloat16)


def table_of(stats):
    parts = stats.astype(jnp.float32)
    rows = parts[0:4] + (parts[4:8] + parts[8:12])
    rows = jnp.concatenate([rows, jnp.zeros((HEAD_DIM - 4, HEAD_DIM), jnp.float32)], axis=0)
    return jnp.transpose(rows)[:TOKENS]


def normed(values, tangent, columns, which, gain):
    inverse = columns[:, 2 * which : 2 * which + 1]
    cross = columns[:, 2 * which + 1 : 2 * which + 2]
    cube = inverse * inverse * inverse
    values = values.astype(jnp.float32)
    tangent = tangent.astype(jnp.float32)
    gain = gain.astype(jnp.float32)
    rows = (values * inverse * gain).astype(jnp.bfloat16)
    return rows, ((tangent * inverse - values * cube * cross) * gain).astype(jnp.bfloat16)


def copy_columns(chip, arrays, out, place):
    target = jnp.bitwise_xor(chip, STEPS[place])
    for index, array in enumerate(arrays):
        for head in range(HEADS_PER_CHIP):
            column = pl.multiple_of(target * FEATURES + head * HEAD_DIM, HEAD_DIM)
            row = index * BLOCK + head * TOKENS
            out[row : row + TOKENS, :] = array[:, pl.ds(column, HEAD_DIM)]


def pack_kernel(chip_ref, *refs):
    arrays, outs, late = refs[:ARRAYS], refs[ARRAYS : ARRAYS + CHIPS], refs[ARRAYS + CHIPS :]
    stats = statistics((arrays[4:], arrays[:2]))
    for place, out in enumerate(outs):
        kept = arrays[:4] if place in LATE else arrays
        copy_columns(chip_ref[0], kept, out, place)
        out[len(kept) * BLOCK :, :] = stats
    for place, out in zip(LATE, late):
        copy_columns(chip_ref[0], arrays[4:], out, place)


def norm_kernel(gain_ref, *refs):
    blocks, (kv_ref, table_ref) = refs[:CHIPS], refs[CHIPS:]
    for place, block in enumerate(blocks):
        where = pl.ds(place * TOKENS, TOKENS)
        columns = table_of(block[block.shape[0] - STAT_ROWS :, :])
        table_ref[where, :] = columns
        for head in range(HEADS_PER_CHIP):
            rows = [block[i * BLOCK + head * TOKENS :][:TOKENS] for i in range(4)]
            rows[:2] = normed(rows[0], rows[1], columns, 1, gain_ref[1, head : head + 1, :])
            for index in range(4):
                kv_ref[index, head, where, :] = rows[index]


CONTRACT = (((1,), (1,)), ((), ()))


def attend_kernel(places, gain_ref, table_ref, own_ref, other_ref, *refs):
    blocks, outs = refs[: len(places)], refs[len(places) :]
    factor = HEAD_DIM**-0.5
    for head in range(HEADS_PER_CHIP):

        def both(index, head=head):
            return jnp.concatenate([own_ref[index, head], other_ref[index, head]], axis=0)

        keys, keys_dot, values, values_dot = both(0), both(1), both(2), both(3)
        keys_pair = jnp.concatenate([keys, keys_dot], axis=1)
        values_pair = jnp.concatenate([values, values_dot], axis=1)
        token = slice(head * TOKENS, (head + 1) * TOKENS)
        tangent_token = slice(BLOCK + head * TOKENS, BLOCK + (head + 1) * TOKENS)
        pairs = []
        for place, block in zip(places, blocks):
            first = block.shape[0] - 2 * BLOCK if place in LATE else 4 * BLOCK
            rows = [block[first + i * BLOCK + head * TOKENS :][:TOKENS] for i in range(2)]
            columns = table_ref[place * TOKENS : (place + 1) * TOKENS, :]
            pairs.append(normed(*rows, columns, 0, gain_ref[0, head : head + 1, :]))
        queries = jnp.concatenate([pair[0] for pair in pairs], axis=0)
        queries_dot = jnp.concatenate([pair[1] for pair in pairs], axis=0)
        queries_pair = jnp.concatenate([queries_dot, queries], axis=1)
        scores = lax.dot_general(queries, keys, CONTRACT, preferred_element_type=jnp.float32)
        scores_dot = lax.dot_general(
            queries_pair, keys_pair, CONTRACT, preferred_element_type=jnp.float32
        )
        peak = jnp.max(scores, axis=1, keepdims=True)
        exponent = jnp.exp2((scores - peak) * (factor * LOG2E))
        scale = 1.0 / jnp.sum(exponent, axis=1, keepdims=True)
        weights = exponent * scale
        mean = jnp.sum(weights * scores_dot, axis=1, keepdims=True)
        weights_dot = (weights * factor) * (scores_dot - mean)
        probs = weights.astype(jnp.bfloat16)
        probs_dot = weights_dot.astype(jnp.bfloat16)
        pair = jnp.dot(probs, values_pair, preferred_element_type=jnp.float32)
        output_dot = jnp.dot(probs_dot, values, preferred_element_type=jnp.float32)
        output = pair[:, :HEAD_DIM].astype(jnp.bfloat16)
        output_dot = (output_dot + pair[:, HEAD_DIM:]).astype(jnp.bfloat16)
        for index, out in enumerate(outs):
            rows = slice(index * TOKENS, (index + 1) * TOKENS)
            out[token, :] = output[rows]
            out[tangent_token, :] = output_dot[rows]


def unpack_kernel(chip_ref, *refs):
    blocks, outs = refs[:CHIPS], refs[CHIPS:]
    for block, place in zip(blocks, ORDER):
        source = jnp.bitwise_xor(chip_ref[0], STEPS[place])
        for index, out in enumerate(outs):
            for head in range(HEADS_PER_CHIP):
                column = pl.multiple_of(source * FEATURES + head * HEAD_DIM, HEAD_DIM)
                row = index * BLOCK + head * TOKENS
                out[:, pl.ds(column, HEAD_DIM)] = block[row : row + TOKENS, :]


def exchange(block, step):
    pairs = [(place, place ^ (2 * step)) for place in range(2 * CHIPS)]
    return lax.ppermute(block, "ctx", pairs)


def swap(block):
    return lax.ppermute(block, "ctx", [(place, place ^ 1) for place in range(2 * CHIPS)])


def after(block, other):
    return lax.optimization_barrier((block, other))


def send(blocks, places=range(CHIPS)):
    steps = [STEPS[place] for place in places]
    return [exchange(block, step) if step else block for block, step in zip(blocks, steps)]


def gather_gains(gains, chip):
    shards = lax.axis_size("dp")
    gains = jnp.broadcast_to(gains[None], (shards, *gains.shape))
    gains = lax.all_to_all(gains, "dp", 0, 0, tiled=True)
    gains = jnp.moveaxis(gains, 0, 1).reshape(2, -1, HEAD_DIM)
    return lax.dynamic_slice_in_dim(gains, chip * HEADS_PER_CHIP, HEADS_PER_CHIP, axis=1)


def local(q, k, v, qd, kd, vd, query_gain, key_gain):
    q, k, v, qd, kd, vd = (array[0] for array in (q, k, v, qd, kd, vd))
    chip = (lax.axis_index("ctx") // 2).astype(jnp.int32)
    chip_ref = chip.reshape(1)

    sizes = [4 if place in LATE else ARRAYS for place in range(CHIPS)]
    blocks = pl.pallas_call(
        pack_kernel,
        out_shape=[shape(size * BLOCK + STAT_ROWS, HEAD_DIM) for size in sizes]
        + [shape(2 * BLOCK, HEAD_DIM)] * len(LATE),
        in_specs=smem() + vmem(ARRAYS),
        out_specs=vmem(CHIPS + len(LATE)),
        compiler_params=params(PACK_MIB),
        name="pack",
    )(chip_ref, k, kd, v, vd, q, qd)
    blocks, late = blocks[:CHIPS], blocks[CHIPS:]
    arrived = send(blocks[:5])
    for place, gate in zip(LATE, (1, 3)):
        block, arrived[gate] = after(blocks[place], arrived[gate])
        arrived.append(exchange(block, STEPS[place]))
    arrived.append(blocks[7])
    late = [exchange(block, STEPS[place]) for block, place in zip(late, LATE)]

    gains = jnp.stack([query_gain, key_gain])
    gains, arrived[3] = after(gains, arrived[3])
    gains = gather_gains(gains, chip)

    many = CHIPS * TOKENS
    own, table = pl.pallas_call(
        norm_kernel,
        out_shape=[
            shape(4, HEADS_PER_CHIP, many, HEAD_DIM),
            shape(many, HEAD_DIM, dtype=jnp.float32),
        ],
        in_specs=vmem(1 + CHIPS),
        out_specs=vmem(2),
        compiler_params=params(16),
        name="norm",
    )(gains, *arrived)
    other = swap(own)

    def attend(places, blocks):
        return pl.pallas_call(
            functools.partial(attend_kernel, places),
            out_shape=[shape(2 * BLOCK, HEAD_DIM)] * len(places),
            in_specs=vmem(4 + len(places)),
            out_specs=vmem(len(places)),
            compiler_params=params(32),
            name="attend",
        )(gains, table, own, other, *blocks)

    outs = dict(zip(EARLY, attend(EARLY, [arrived[place] for place in EARLY])))
    outs.update(zip(LATE, attend(LATE, late)))
    back = dict(zip(ORDER, send([outs[place] for place in ORDER], ORDER)))

    rows, width = q.shape
    attended, attended_tangent = pl.pallas_call(
        unpack_kernel,
        out_shape=[shape(rows, width)] * 2,
        in_specs=smem() + vmem(CHIPS),
        out_specs=vmem(2),
        compiler_params=params(16),
        name="unpack",
    )(chip_ref, *[back[place] for place in ORDER])
    return attended[None], attended_tangent[None]


def solution(mesh):
    rows = P("dp", "ctx", None)
    return jax.shard_map(
        local,
        mesh=mesh,
        in_specs=(rows,) * 6 + (P("dp"), P("dp")),
        out_specs=(rows, rows),
        check_vma=False,
    )
```

```python
import functools

import jax
import jax.numpy as jnp
from jax import lax
from jax.experimental import pallas as pl
from jax.experimental.pallas import tpu as pltpu
from jax.sharding import PartitionSpec as P

HEAD_DIM = 128
CHIPS = 8
HEADS_PER_CHIP = 4
TOKENS = 64
FEATURES = HEADS_PER_CHIP * HEAD_DIM
BLOCK = HEADS_PER_CHIP * TOKENS
STAT_ROWS = 16
ARRAYS = 6
STEPS = (5, 1, 6, 3, 2, 4, 7, 0)
GATES = (None, None, None, None, None, 1, 3, None)
GAINS_GATE = 3
LATE = (5, 6)
EARLY = (0, 1, 2, 3, 4, 7)
ORDER = (0, 2, 5, 6, 1, 3, 4, 7)
PACK_MIB = 56
LOG2E = 1.4426950408889634
MIB = 1024 * 1024


def vmem(count):
    return [pl.BlockSpec(memory_space=pltpu.VMEM)] * count


def smem():
    return [pl.BlockSpec(memory_space=pltpu.SMEM)]


def params(mib):
    return pltpu.CompilerParams(vmem_limit_bytes=mib * MIB)


def shape(*sizes, dtype=jnp.bfloat16):
    return jax.ShapeDtypeStruct(sizes, dtype)


def statistics(pairs):
    columns = []
    for values_ref, tangent_ref in pairs:
        square = jnp.zeros((TOKENS, HEAD_DIM), jnp.float32)
        cross = jnp.zeros((TOKENS, HEAD_DIM), jnp.float32)
        width = values_ref.shape[1]
        for start in range(0, width, HEAD_DIM):
            values = values_ref[:, start : start + HEAD_DIM].astype(jnp.float32)
            tangent = tangent_ref[:, start : start + HEAD_DIM].astype(jnp.float32)
            square += values * values
            cross += values * tangent
        mean_square = jnp.sum(square, axis=1, keepdims=True) / width
        columns.append(lax.rsqrt(mean_square + 1e-06))
        columns.append(jnp.sum(cross, axis=1, keepdims=True) / width)
    lane = lax.broadcasted_iota(jnp.int32, (TOKENS, HEAD_DIM), 1)
    table = jnp.zeros((TOKENS, HEAD_DIM), jnp.float32)
    for index, column in enumerate(columns):
        rest = column
        for part in range(3):
            piece = rest.astype(jnp.bfloat16).astype(jnp.float32)
            rest = rest - piece
            table = jnp.where(lane == part * 4 + index, piece, table)
    table = jnp.concatenate([table, jnp.zeros((HEAD_DIM - TOKENS, HEAD_DIM), jnp.float32)], axis=0)
    return jnp.transpose(table)[:STAT_ROWS].astype(jnp.bfloat16)


def table_of(stats):
    parts = stats.astype(jnp.float32)
    rows = parts[0:4] + (parts[4:8] + parts[8:12])
    rows = jnp.concatenate([rows, jnp.zeros((HEAD_DIM - 4, HEAD_DIM), jnp.float32)], axis=0)
    return jnp.transpose(rows)[:TOKENS]


def normed(values, tangent, columns, which, gain):
    inverse = columns[:, 2 * which : 2 * which + 1]
    cross = columns[:, 2 * which + 1 : 2 * which + 2]
    cube = inverse * inverse * inverse
    values = values.astype(jnp.float32)
    tangent = tangent.astype(jnp.float32)
    gain = gain.astype(jnp.float32)
    rows = (values * inverse * gain).astype(jnp.bfloat16)
    return rows, ((tangent * inverse - values * cube * cross) * gain).astype(jnp.bfloat16)


def copy_columns(chip, arrays, out, place):
    target = jnp.bitwise_xor(chip, STEPS[place])
    for index, array in enumerate(arrays):
        for head in range(HEADS_PER_CHIP):
            column = pl.multiple_of(target * FEATURES + head * HEAD_DIM, HEAD_DIM)
            row = index * BLOCK + head * TOKENS
            out[row : row + TOKENS, :] = array[:, pl.ds(column, HEAD_DIM)]


def pack_kernel(chip_ref, *refs):
    arrays, outs, late = refs[:ARRAYS], refs[ARRAYS : ARRAYS + CHIPS], refs[ARRAYS + CHIPS :]
    stats = statistics((arrays[4:], arrays[:2]))
    for place, out in enumerate(outs):
        kept = arrays[:4] if place in LATE else arrays
        copy_columns(chip_ref[0], kept, out, place)
        out[len(kept) * BLOCK :, :] = stats
    for place, out in zip(LATE, late):
        copy_columns(chip_ref[0], arrays[4:], out, place)


def norm_kernel(gain_ref, *refs):
    blocks, (kv_ref, table_ref) = refs[:CHIPS], refs[CHIPS:]
    for place, block in enumerate(blocks):
        where = pl.ds(place * TOKENS, TOKENS)
        columns = table_of(block[block.shape[0] - STAT_ROWS :, :])
        table_ref[where, :] = columns
        for head in range(HEADS_PER_CHIP):
            rows = [block[i * BLOCK + head * TOKENS :][:TOKENS] for i in range(4)]
            rows[:2] = normed(rows[0], rows[1], columns, 1, gain_ref[1, head : head + 1, :])
            for index in range(4):
                kv_ref[index, head, where, :] = rows[index]


CONTRACT = (((1,), (1,)), ((), ()))


def attend_kernel(places, gain_ref, table_ref, own_ref, other_ref, *refs):
    blocks, outs = refs[: len(places)], refs[len(places) :]
    factor = HEAD_DIM**-0.5
    for head in range(HEADS_PER_CHIP):

        def both(index, head=head):
            return jnp.concatenate([own_ref[index, head], other_ref[index, head]], axis=0)

        keys, keys_dot, values, values_dot = both(0), both(1), both(2), both(3)
        keys_pair = jnp.concatenate([keys, keys_dot], axis=1)
        values_pair = jnp.concatenate([values, values_dot], axis=1)
        token = slice(head * TOKENS, (head + 1) * TOKENS)
        tangent_token = slice(BLOCK + head * TOKENS, BLOCK + (head + 1) * TOKENS)
        pairs = []
        for place, block in zip(places, blocks):
            first = block.shape[0] - 2 * BLOCK if place in LATE else 4 * BLOCK
            rows = [block[first + i * BLOCK + head * TOKENS :][:TOKENS] for i in range(2)]
            columns = table_ref[place * TOKENS : (place + 1) * TOKENS, :]
            pairs.append(normed(*rows, columns, 0, gain_ref[0, head : head + 1, :]))
        queries = jnp.concatenate([pair[0] for pair in pairs], axis=0)
        queries_dot = jnp.concatenate([pair[1] for pair in pairs], axis=0)
        queries_pair = jnp.concatenate([queries_dot, queries], axis=1)
        scores = lax.dot_general(queries, keys, CONTRACT, preferred_element_type=jnp.float32)
        scores_dot = lax.dot_general(
            queries_pair, keys_pair, CONTRACT, preferred_element_type=jnp.float32
        )
        peak = jnp.max(scores, axis=1, keepdims=True)
        exponent = jnp.exp2((scores - peak) * (factor * LOG2E))
        scale = 1.0 / jnp.sum(exponent, axis=1, keepdims=True)
        weights = exponent * scale
        mean = jnp.sum(weights * scores_dot, axis=1, keepdims=True)
        weights_dot = (weights * factor) * (scores_dot - mean)
        probs = weights.astype(jnp.bfloat16)
        probs_dot = weights_dot.astype(jnp.bfloat16)
        pair = jnp.dot(probs, values_pair, preferred_element_type=jnp.float32)
        output_dot = jnp.dot(probs_dot, values, preferred_element_type=jnp.float32)
        output = pair[:, :HEAD_DIM].astype(jnp.bfloat16)
        output_dot = (output_dot + pair[:, HEAD_DIM:]).astype(jnp.bfloat16)
        for index, out in enumerate(outs):
            rows = slice(index * TOKENS, (index + 1) * TOKENS)
            out[token, :] = output[rows]
            out[tangent_token, :] = output_dot[rows]


def unpack_kernel(chip_ref, *refs):
    blocks, outs = refs[:CHIPS], refs[CHIPS:]
    for block, place in zip(blocks, ORDER):
        source = jnp.bitwise_xor(chip_ref[0], STEPS[place])
        for index, out in enumerate(outs):
            for head in range(HEADS_PER_CHIP):
                column = pl.multiple_of(source * FEATURES + head * HEAD_DIM, HEAD_DIM)
                row = index * BLOCK + head * TOKENS
                out[:, pl.ds(column, HEAD_DIM)] = block[row : row + TOKENS, :]


def exchange(block, step):
    pairs = [(place, place ^ (2 * step)) for place in range(2 * CHIPS)]
    return lax.ppermute(block, "ctx", pairs)


def swap(block):
    return lax.ppermute(block, "ctx", [(place, place ^ 1) for place in range(2 * CHIPS)])


def after(block, other):
    return lax.optimization_barrier((block, other))


def send(blocks, places=range(CHIPS)):
    steps = [STEPS[place] for place in places]
    return [exchange(block, step) if step else block for block, step in zip(blocks, steps)]


def gather_gains(gains, chip):
    shards = lax.axis_size("dp")
    gains = jnp.broadcast_to(gains[None], (shards, *gains.shape))
    gains = lax.all_to_all(gains, "dp", 0, 0, tiled=True)
    gains = jnp.moveaxis(gains, 0, 1).reshape(2, -1, HEAD_DIM)
    return lax.dynamic_slice_in_dim(gains, chip * HEADS_PER_CHIP, HEADS_PER_CHIP, axis=1)


def local(q, k, v, qd, kd, vd, query_gain, key_gain):
    q, k, v, qd, kd, vd = (array[0] for array in (q, k, v, qd, kd, vd))
    chip = (lax.axis_index("ctx") // 2).astype(jnp.int32)
    chip_ref = chip.reshape(1)

    sizes = [4 if place in LATE else ARRAYS for place in range(CHIPS)]
    blocks = pl.pallas_call(
        pack_kernel,
        out_shape=[shape(size * BLOCK + STAT_ROWS, HEAD_DIM) for size in sizes]
        + [shape(2 * BLOCK, HEAD_DIM)] * len(LATE),
        in_specs=smem() + vmem(ARRAYS),
        out_specs=vmem(CHIPS + len(LATE)),
        compiler_params=params(PACK_MIB),
        name="pack",
    )(chip_ref, k, kd, v, vd, q, qd)
    blocks, late = blocks[:CHIPS], blocks[CHIPS:]
    arrived = []
    for place, gate in enumerate(GATES):
        block = blocks[place]
        if gate is not None:
            block, arrived[gate] = after(block, arrived[gate])
        arrived.append(exchange(block, STEPS[place]) if STEPS[place] else block)
    late = [exchange(block, STEPS[place]) for block, place in zip(late, LATE)]

    gains = jnp.stack([query_gain, key_gain])
    gains, arrived[GAINS_GATE] = after(gains, arrived[GAINS_GATE])
    gains = gather_gains(gains, chip)

    many = CHIPS * TOKENS
    own, table = pl.pallas_call(
        norm_kernel,
        out_shape=[
            shape(4, HEADS_PER_CHIP, many, HEAD_DIM),
            shape(many, HEAD_DIM, dtype=jnp.float32),
        ],
        in_specs=vmem(1 + CHIPS),
        out_specs=vmem(2),
        compiler_params=params(16),
        name="norm",
    )(gains, *arrived)
    other = swap(own)

    def attend(places, blocks):
        return pl.pallas_call(
            functools.partial(attend_kernel, places),
            out_shape=[shape(2 * BLOCK, HEAD_DIM)] * len(places),
            in_specs=vmem(4 + len(places)),
            out_specs=vmem(len(places)),
            compiler_params=params(32),
            name="attend",
        )(gains, table, own, other, *blocks)

    outs = dict(zip(EARLY, attend(EARLY, [arrived[place] for place in EARLY])))
    outs.update(zip(LATE, attend(LATE, late)))
    back = dict(zip(ORDER, send([outs[place] for place in ORDER], ORDER)))

    rows, width = q.shape
    attended, attended_tangent = pl.pallas_call(
        unpack_kernel,
        out_shape=[shape(rows, width)] * 2,
        in_specs=smem() + vmem(CHIPS),
        out_specs=vmem(2),
        compiler_params=params(16),
        name="unpack",
    )(chip_ref, *[back[place] for place in ORDER])
    return attended[None], attended_tangent[None]


def solution(mesh):
    rows = P("dp", "ctx", None)
    return jax.shard_map(
        local,
        mesh=mesh,
        in_specs=(rows,) * 6 + (P("dp"), P("dp")),
        out_specs=(rows, rows),
        check_vma=False,
    )
```

```python
import functools

import jax
import jax.numpy as jnp
from jax import lax
from jax.experimental import pallas as pl
from jax.experimental.pallas import tpu as pltpu
from jax.sharding import PartitionSpec as P

HEAD_DIM = 128
CHIPS = 8
HEADS_PER_CHIP = 4
TOKENS = 64
FEATURES = HEADS_PER_CHIP * HEAD_DIM
BLOCK = HEADS_PER_CHIP * TOKENS
STAT_ROWS = 16
ARRAYS = 6
STEPS = (4, 1, 5, 2, 3, 7, 6, 0)
GATES = (None, None, None, None, None, 1, 3, None)
GAINS_GATE = 3
LATE = (5, 6)
EARLY = (0, 1, 2, 3, 4, 7)
ORDER = (0, 2, 5, 6, 1, 3, 4, 7)
PACK_MIB = 56
LOG2E = 1.4426950408889634
MIB = 1024 * 1024


def vmem(count):
    return [pl.BlockSpec(memory_space=pltpu.VMEM)] * count


def smem():
    return [pl.BlockSpec(memory_space=pltpu.SMEM)]


def params(mib):
    return pltpu.CompilerParams(vmem_limit_bytes=mib * MIB)


def shape(*sizes, dtype=jnp.bfloat16):
    return jax.ShapeDtypeStruct(sizes, dtype)


def statistics(pairs):
    columns = []
    for values_ref, tangent_ref in pairs:
        square = jnp.zeros((TOKENS, HEAD_DIM), jnp.float32)
        cross = jnp.zeros((TOKENS, HEAD_DIM), jnp.float32)
        width = values_ref.shape[1]
        for start in range(0, width, HEAD_DIM):
            values = values_ref[:, start : start + HEAD_DIM].astype(jnp.float32)
            tangent = tangent_ref[:, start : start + HEAD_DIM].astype(jnp.float32)
            square += values * values
            cross += values * tangent
        mean_square = jnp.sum(square, axis=1, keepdims=True) / width
        columns.append(lax.rsqrt(mean_square + 1e-06))
        columns.append(jnp.sum(cross, axis=1, keepdims=True) / width)
    lane = lax.broadcasted_iota(jnp.int32, (TOKENS, HEAD_DIM), 1)
    table = jnp.zeros((TOKENS, HEAD_DIM), jnp.float32)
    for index, column in enumerate(columns):
        rest = column
        for part in range(3):
            piece = rest.astype(jnp.bfloat16).astype(jnp.float32)
            rest = rest - piece
            table = jnp.where(lane == part * 4 + index, piece, table)
    table = jnp.concatenate([table, jnp.zeros((HEAD_DIM - TOKENS, HEAD_DIM), jnp.float32)], axis=0)
    return jnp.transpose(table)[:STAT_ROWS].astype(jnp.bfloat16)


def table_of(stats):
    parts = stats.astype(jnp.float32)
    rows = parts[0:4] + (parts[4:8] + parts[8:12])
    rows = jnp.concatenate([rows, jnp.zeros((HEAD_DIM - 4, HEAD_DIM), jnp.float32)], axis=0)
    return jnp.transpose(rows)[:TOKENS]


def normed(values, tangent, columns, which, gain):
    inverse = columns[:, 2 * which : 2 * which + 1]
    cross = columns[:, 2 * which + 1 : 2 * which + 2]
    cube = inverse * inverse * inverse
    values = values.astype(jnp.float32)
    tangent = tangent.astype(jnp.float32)
    gain = gain.astype(jnp.float32)
    rows = (values * inverse * gain).astype(jnp.bfloat16)
    return rows, ((tangent * inverse - values * cube * cross) * gain).astype(jnp.bfloat16)


def copy_columns(chip, arrays, out, place):
    target = jnp.bitwise_xor(chip, STEPS[place])
    for index, array in enumerate(arrays):
        for head in range(HEADS_PER_CHIP):
            column = pl.multiple_of(target * FEATURES + head * HEAD_DIM, HEAD_DIM)
            row = index * BLOCK + head * TOKENS
            out[row : row + TOKENS, :] = array[:, pl.ds(column, HEAD_DIM)]


def pack_kernel(chip_ref, *refs):
    arrays, outs, late = refs[:ARRAYS], refs[ARRAYS : ARRAYS + CHIPS], refs[ARRAYS + CHIPS :]
    stats = statistics((arrays[4:], arrays[:2]))
    for place, out in enumerate(outs):
        kept = arrays[:4] if place in LATE else arrays
        copy_columns(chip_ref[0], kept, out, place)
        out[len(kept) * BLOCK :, :] = stats
    for place, out in zip(LATE, late):
        copy_columns(chip_ref[0], arrays[4:], out, place)


def norm_kernel(gain_ref, *refs):
    blocks, (kv_ref, table_ref) = refs[:CHIPS], refs[CHIPS:]
    for place, block in enumerate(blocks):
        where = pl.ds(place * TOKENS, TOKENS)
        columns = table_of(block[block.shape[0] - STAT_ROWS :, :])
        table_ref[where, :] = columns
        for head in range(HEADS_PER_CHIP):
            rows = [block[i * BLOCK + head * TOKENS :][:TOKENS] for i in range(4)]
            rows[:2] = normed(rows[0], rows[1], columns, 1, gain_ref[1, head : head + 1, :])
            for index in range(4):
                kv_ref[index, head, where, :] = rows[index]


CONTRACT = (((1,), (1,)), ((), ()))


def attend_kernel(places, gain_ref, table_ref, own_ref, other_ref, *refs):
    blocks, outs = refs[: len(places)], refs[len(places) :]
    factor = HEAD_DIM**-0.5
    for head in range(HEADS_PER_CHIP):

        def both(index, head=head):
            return jnp.concatenate([own_ref[index, head], other_ref[index, head]], axis=0)

        keys, keys_dot, values, values_dot = both(0), both(1), both(2), both(3)
        keys_pair = jnp.concatenate([keys, keys_dot], axis=1)
        values_pair = jnp.concatenate([values, values_dot], axis=1)
        token = slice(head * TOKENS, (head + 1) * TOKENS)
        tangent_token = slice(BLOCK + head * TOKENS, BLOCK + (head + 1) * TOKENS)
        pairs = []
        for place, block in zip(places, blocks):
            first = block.shape[0] - 2 * BLOCK if place in LATE else 4 * BLOCK
            rows = [block[first + i * BLOCK + head * TOKENS :][:TOKENS] for i in range(2)]
            columns = table_ref[place * TOKENS : (place + 1) * TOKENS, :]
            pairs.append(normed(*rows, columns, 0, gain_ref[0, head : head + 1, :]))
        queries = jnp.concatenate([pair[0] for pair in pairs], axis=0)
        queries_dot = jnp.concatenate([pair[1] for pair in pairs], axis=0)
        queries_pair = jnp.concatenate([queries_dot, queries], axis=1)
        scores = lax.dot_general(queries, keys, CONTRACT, preferred_element_type=jnp.float32)
        scores_dot = lax.dot_general(
            queries_pair, keys_pair, CONTRACT, preferred_element_type=jnp.float32
        )
        peak = jnp.max(scores, axis=1, keepdims=True)
        exponent = jnp.exp2((scores - peak) * (factor * LOG2E))
        scale = 1.0 / jnp.sum(exponent, axis=1, keepdims=True)
        weights = exponent * scale
        mean = jnp.sum(weights * scores_dot, axis=1, keepdims=True)
        weights_dot = (weights * factor) * (scores_dot - mean)
        probs = weights.astype(jnp.bfloat16)
        probs_dot = weights_dot.astype(jnp.bfloat16)
        pair = jnp.dot(probs, values_pair, preferred_element_type=jnp.float32)
        output_dot = jnp.dot(probs_dot, values, preferred_element_type=jnp.float32)
        output = pair[:, :HEAD_DIM].astype(jnp.bfloat16)
        output_dot = (output_dot + pair[:, HEAD_DIM:]).astype(jnp.bfloat16)
        for index, out in enumerate(outs):
            rows = slice(index * TOKENS, (index + 1) * TOKENS)
            out[token, :] = output[rows]
            out[tangent_token, :] = output_dot[rows]


def unpack_kernel(chip_ref, *refs):
    blocks, outs = refs[:CHIPS], refs[CHIPS:]
    for block, place in zip(blocks, ORDER):
        source = jnp.bitwise_xor(chip_ref[0], STEPS[place])
        for index, out in enumerate(outs):
            for head in range(HEADS_PER_CHIP):
                column = pl.multiple_of(source * FEATURES + head * HEAD_DIM, HEAD_DIM)
                row = index * BLOCK + head * TOKENS
                out[:, pl.ds(column, HEAD_DIM)] = block[row : row + TOKENS, :]


def exchange(block, step):
    pairs = [(place, place ^ (2 * step)) for place in range(2 * CHIPS)]
    return lax.ppermute(block, "ctx", pairs)


def swap(block):
    return lax.ppermute(block, "ctx", [(place, place ^ 1) for place in range(2 * CHIPS)])


def after(block, other):
    return lax.optimization_barrier((block, other))


def send(blocks, places=range(CHIPS)):
    steps = [STEPS[place] for place in places]
    return [exchange(block, step) if step else block for block, step in zip(blocks, steps)]


def gather_gains(gains, chip):
    shards = lax.axis_size("dp")
    gains = jnp.broadcast_to(gains[None], (shards, *gains.shape))
    gains = lax.all_to_all(gains, "dp", 0, 0, tiled=True)
    gains = jnp.moveaxis(gains, 0, 1).reshape(2, -1, HEAD_DIM)
    return lax.dynamic_slice_in_dim(gains, chip * HEADS_PER_CHIP, HEADS_PER_CHIP, axis=1)


def local(q, k, v, qd, kd, vd, query_gain, key_gain):
    q, k, v, qd, kd, vd = (array[0] for array in (q, k, v, qd, kd, vd))
    chip = (lax.axis_index("ctx") // 2).astype(jnp.int32)
    chip_ref = chip.reshape(1)

    sizes = [4 if place in LATE else ARRAYS for place in range(CHIPS)]
    blocks = pl.pallas_call(
        pack_kernel,
        out_shape=[shape(size * BLOCK + STAT_ROWS, HEAD_DIM) for size in sizes]
        + [shape(2 * BLOCK, HEAD_DIM)] * len(LATE),
        in_specs=smem() + vmem(ARRAYS),
        out_specs=vmem(CHIPS + len(LATE)),
        compiler_params=params(PACK_MIB),
        name="pack",
    )(chip_ref, k, kd, v, vd, q, qd)
    blocks, late = blocks[:CHIPS], blocks[CHIPS:]
    arrived = []
    for place, gate in enumerate(GATES):
        block = blocks[place]
        if gate is not None:
            block, arrived[gate] = after(block, arrived[gate])
        arrived.append(exchange(block, STEPS[place]) if STEPS[place] else block)
    late = [exchange(block, STEPS[place]) for block, place in zip(late, LATE)]

    gains = jnp.stack([query_gain, key_gain])
    gains, arrived[GAINS_GATE] = after(gains, arrived[GAINS_GATE])
    gains = gather_gains(gains, chip)

    many = CHIPS * TOKENS
    own, table = pl.pallas_call(
        norm_kernel,
        out_shape=[
            shape(4, HEADS_PER_CHIP, many, HEAD_DIM),
            shape(many, HEAD_DIM, dtype=jnp.float32),
        ],
        in_specs=vmem(1 + CHIPS),
        out_specs=vmem(2),
        compiler_params=params(16),
        name="norm",
    )(gains, *arrived)
    other = swap(own)

    def attend(places, blocks):
        return pl.pallas_call(
            functools.partial(attend_kernel, places),
            out_shape=[shape(2 * BLOCK, HEAD_DIM)] * len(places),
            in_specs=vmem(4 + len(places)),
            out_specs=vmem(len(places)),
            compiler_params=params(32),
            name="attend",
        )(gains, table, own, other, *blocks)

    outs = dict(zip(EARLY, attend(EARLY, [arrived[place] for place in EARLY])))
    outs.update(zip(LATE, attend(LATE, late)))
    back = dict(zip(ORDER, send([outs[place] for place in ORDER], ORDER)))

    rows, width = q.shape
    attended, attended_tangent = pl.pallas_call(
        unpack_kernel,
        out_shape=[shape(rows, width)] * 2,
        in_specs=smem() + vmem(CHIPS),
        out_specs=vmem(2),
        compiler_params=params(16),
        name="unpack",
    )(chip_ref, *[back[place] for place in ORDER])
    return attended[None], attended_tangent[None]


def solution(mesh):
    rows = P("dp", "ctx", None)
    return jax.shard_map(
        local,
        mesh=mesh,
        in_specs=(rows,) * 6 + (P("dp"), P("dp")),
        out_specs=(rows, rows),
        check_vma=False,
    )
```

```python
import functools

import jax
import jax.numpy as jnp
from jax import lax
from jax.experimental import pallas as pl
from jax.experimental.pallas import tpu as pltpu
from jax.sharding import PartitionSpec as P

HEAD_DIM = 128
CHIPS = 8
HEADS_PER_CHIP = 4
TOKENS = 64
FEATURES = HEADS_PER_CHIP * HEAD_DIM
BLOCK = HEADS_PER_CHIP * TOKENS
STAT_ROWS = 16
ARRAYS = 6
STEPS = (4, 1, 5, 2, 3, 7, 6, 0)
GATES = (None, None, None, None, None, 1, 3, None)
GAINS_GATE = 3
LATE = (5, 6)
EARLY = (0, 1, 2, 3, 4, 7)
ORDER = (0, 2, 5, 6, 1, 3, 4, 7)
PACK_MIB = 56
LOG2E = 1.4426950408889634
MIB = 1024 * 1024


def vmem(count):
    return [pl.BlockSpec(memory_space=pltpu.VMEM)] * count


def smem():
    return [pl.BlockSpec(memory_space=pltpu.SMEM)]


def params(mib):
    return pltpu.CompilerParams(vmem_limit_bytes=mib * MIB)


def shape(*sizes, dtype=jnp.bfloat16):
    return jax.ShapeDtypeStruct(sizes, dtype)


def statistics(pairs):
    columns = []
    for values_ref, tangent_ref in pairs:
        square = jnp.zeros((TOKENS, HEAD_DIM), jnp.float32)
        cross = jnp.zeros((TOKENS, HEAD_DIM), jnp.float32)
        width = values_ref.shape[1]
        for start in range(0, width, HEAD_DIM):
            values = values_ref[:, start : start + HEAD_DIM].astype(jnp.float32)
            tangent = tangent_ref[:, start : start + HEAD_DIM].astype(jnp.float32)
            square += values * values
            cross += values * tangent
        mean_square = jnp.sum(square, axis=1, keepdims=True) / width
        columns.append(lax.rsqrt(mean_square + 1e-06))
        columns.append(jnp.sum(cross, axis=1, keepdims=True) / width)
    lane = lax.broadcasted_iota(jnp.int32, (TOKENS, HEAD_DIM), 1)
    table = jnp.zeros((TOKENS, HEAD_DIM), jnp.float32)
    for index, column in enumerate(columns):
        rest = column
        for part in range(3):
            piece = rest.astype(jnp.bfloat16).astype(jnp.float32)
            rest = rest - piece
            table = jnp.where(lane == part * 4 + index, piece, table)
    table = jnp.concatenate([table, jnp.zeros((HEAD_DIM - TOKENS, HEAD_DIM), jnp.float32)], axis=0)
    return jnp.transpose(table)[:STAT_ROWS].astype(jnp.bfloat16)


def table_of(stats):
    parts = stats.astype(jnp.float32)
    rows = parts[0:4] + (parts[4:8] + parts[8:12])
    rows = jnp.concatenate([rows, jnp.zeros((HEAD_DIM - 4, HEAD_DIM), jnp.float32)], axis=0)
    return jnp.transpose(rows)[:TOKENS]


def normed(values, tangent, columns, which, gain):
    inverse = columns[:, 2 * which : 2 * which + 1]
    cross = columns[:, 2 * which + 1 : 2 * which + 2]
    cube = inverse * inverse * inverse
    values = values.astype(jnp.float32)
    tangent = tangent.astype(jnp.float32)
    gain = gain.astype(jnp.float32)
    rows = (values * inverse * gain).astype(jnp.bfloat16)
    return rows, ((tangent * inverse - values * cube * cross) * gain).astype(jnp.bfloat16)


def copy_columns(chip, arrays, out, place):
    target = jnp.bitwise_xor(chip, STEPS[place])
    for index, array in enumerate(arrays):
        for head in range(HEADS_PER_CHIP):
            column = pl.multiple_of(target * FEATURES + head * HEAD_DIM, HEAD_DIM)
            row = index * BLOCK + head * TOKENS
            out[row : row + TOKENS, :] = array[:, pl.ds(column, HEAD_DIM)]


def pack_kernel(chip_ref, *refs):
    sources, refs = refs[:ARRAYS], refs[ARRAYS:]
    count = CHIPS + len(LATE)
    targets, arrays, blocks = refs[:count], refs[count : count + ARRAYS], refs[count + ARRAYS : -2]
    loaded, stored = refs[-2:]
    loads = [
        pltpu.make_async_copy(source, array, loaded.at[index])
        for index, (source, array) in enumerate(zip(sources, arrays))
    ]
    for index in (4, 5, 0, 1, 2, 3):
        loads[index].start()
    for index in (4, 5, 0, 1):
        loads[index].wait()
    stats = statistics((arrays[4:], arrays[:2]))
    for index in (2, 3):
        loads[index].wait()
    stores = []
    for index, (block, target) in enumerate(zip(blocks, targets)):
        if index < CHIPS:
            kept = arrays[:4] if index in LATE else arrays
            copy_columns(chip_ref[0], kept, block, index)
            block[len(kept) * BLOCK :, :] = stats
        else:
            copy_columns(chip_ref[0], arrays[4:], block, LATE[index - CHIPS])
        store = pltpu.make_async_copy(block, target, stored.at[index])
        store.start()
        stores.append(store)
    for store in stores:
        store.wait()


def norm_kernel(gain_ref, *refs):
    blocks, (kv_ref, table_ref) = refs[:CHIPS], refs[CHIPS:]
    for place, block in enumerate(blocks):
        where = pl.ds(place * TOKENS, TOKENS)
        columns = table_of(block[block.shape[0] - STAT_ROWS :, :])
        table_ref[where, :] = columns
        for head in range(HEADS_PER_CHIP):
            rows = [block[i * BLOCK + head * TOKENS :][:TOKENS] for i in range(4)]
            rows[:2] = normed(rows[0], rows[1], columns, 1, gain_ref[1, head : head + 1, :])
            for index in range(4):
                kv_ref[index, head, where, :] = rows[index]


CONTRACT = (((1,), (1,)), ((), ()))


def attend_kernel(places, gain_ref, table_ref, own_ref, other_ref, *refs):
    blocks, outs = refs[: len(places)], refs[len(places) :]
    factor = HEAD_DIM**-0.5
    for head in range(HEADS_PER_CHIP):

        def both(index, head=head):
            return jnp.concatenate([own_ref[index, head], other_ref[index, head]], axis=0)

        keys, keys_dot, values, values_dot = both(0), both(1), both(2), both(3)
        keys_pair = jnp.concatenate([keys, keys_dot], axis=1)
        values_pair = jnp.concatenate([values, values_dot], axis=1)
        token = slice(head * TOKENS, (head + 1) * TOKENS)
        tangent_token = slice(BLOCK + head * TOKENS, BLOCK + (head + 1) * TOKENS)
        pairs = []
        for place, block in zip(places, blocks):
            first = block.shape[0] - 2 * BLOCK if place in LATE else 4 * BLOCK
            rows = [block[first + i * BLOCK + head * TOKENS :][:TOKENS] for i in range(2)]
            columns = table_ref[place * TOKENS : (place + 1) * TOKENS, :]
            pairs.append(normed(*rows, columns, 0, gain_ref[0, head : head + 1, :]))
        queries = jnp.concatenate([pair[0] for pair in pairs], axis=0)
        queries_dot = jnp.concatenate([pair[1] for pair in pairs], axis=0)
        queries_pair = jnp.concatenate([queries_dot, queries], axis=1)
        scores = lax.dot_general(queries, keys, CONTRACT, preferred_element_type=jnp.float32)
        scores_dot = lax.dot_general(
            queries_pair, keys_pair, CONTRACT, preferred_element_type=jnp.float32
        )
        peak = jnp.max(scores, axis=1, keepdims=True)
        exponent = jnp.exp2((scores - peak) * (factor * LOG2E))
        scale = 1.0 / jnp.sum(exponent, axis=1, keepdims=True)
        weights = exponent * scale
        mean = jnp.sum(weights * scores_dot, axis=1, keepdims=True)
        weights_dot = (weights * factor) * (scores_dot - mean)
        probs = weights.astype(jnp.bfloat16)
        probs_dot = weights_dot.astype(jnp.bfloat16)
        pair = jnp.dot(probs, values_pair, preferred_element_type=jnp.float32)
        output_dot = jnp.dot(probs_dot, values, preferred_element_type=jnp.float32)
        output = pair[:, :HEAD_DIM].astype(jnp.bfloat16)
        output_dot = (output_dot + pair[:, HEAD_DIM:]).astype(jnp.bfloat16)
        for index, out in enumerate(outs):
            rows = slice(index * TOKENS, (index + 1) * TOKENS)
            out[token, :] = output[rows]
            out[tangent_token, :] = output_dot[rows]


def unpack_kernel(chip_ref, *refs):
    blocks, outs = refs[:CHIPS], refs[CHIPS:]
    for block, place in zip(blocks, ORDER):
        source = jnp.bitwise_xor(chip_ref[0], STEPS[place])
        for index, out in enumerate(outs):
            for head in range(HEADS_PER_CHIP):
                column = pl.multiple_of(source * FEATURES + head * HEAD_DIM, HEAD_DIM)
                row = index * BLOCK + head * TOKENS
                out[:, pl.ds(column, HEAD_DIM)] = block[row : row + TOKENS, :]


def exchange(block, step):
    pairs = [(place, place ^ (2 * step)) for place in range(2 * CHIPS)]
    return lax.ppermute(block, "ctx", pairs)


def swap(block):
    return lax.ppermute(block, "ctx", [(place, place ^ 1) for place in range(2 * CHIPS)])


def after(block, other):
    return lax.optimization_barrier((block, other))


def send(blocks, places=range(CHIPS)):
    steps = [STEPS[place] for place in places]
    return [exchange(block, step) if step else block for block, step in zip(blocks, steps)]


def gather_gains(gains, chip):
    shards = lax.axis_size("dp")
    gains = jnp.broadcast_to(gains[None], (shards, *gains.shape))
    gains = lax.all_to_all(gains, "dp", 0, 0, tiled=True)
    gains = jnp.moveaxis(gains, 0, 1).reshape(2, -1, HEAD_DIM)
    return lax.dynamic_slice_in_dim(gains, chip * HEADS_PER_CHIP, HEADS_PER_CHIP, axis=1)


def local(q, k, v, qd, kd, vd, query_gain, key_gain):
    q, k, v, qd, kd, vd = (array[0] for array in (q, k, v, qd, kd, vd))
    chip = (lax.axis_index("ctx") // 2).astype(jnp.int32)
    chip_ref = chip.reshape(1)

    sizes = [4 * BLOCK + STAT_ROWS if place in LATE else ARRAYS * BLOCK + STAT_ROWS for place in range(CHIPS)]
    sizes += [2 * BLOCK] * len(LATE)
    arrays = (k, kd, v, vd, q, qd)
    blocks = pl.pallas_call(
        pack_kernel,
        out_shape=[shape(size, HEAD_DIM) for size in sizes],
        in_specs=smem() + [pl.BlockSpec(memory_space=pl.ANY)] * ARRAYS,
        out_specs=[pl.BlockSpec(memory_space=pl.ANY)] * len(sizes),
        scratch_shapes=[pltpu.VMEM(array.shape, array.dtype) for array in arrays]
        + [pltpu.VMEM((size, HEAD_DIM), jnp.bfloat16) for size in sizes]
        + [pltpu.SemaphoreType.DMA((ARRAYS,)), pltpu.SemaphoreType.DMA((len(sizes),))],
        compiler_params=params(PACK_MIB),
        name="pack",
    )(chip_ref, *arrays)
    blocks, late = blocks[:CHIPS], blocks[CHIPS:]
    arrived = []
    for place, gate in enumerate(GATES):
        block = blocks[place]
        if gate is not None:
            block, arrived[gate] = after(block, arrived[gate])
        arrived.append(exchange(block, STEPS[place]) if STEPS[place] else block)
    late = [exchange(block, STEPS[place]) for block, place in zip(late, LATE)]

    gains = jnp.stack([query_gain, key_gain])
    gains, arrived[GAINS_GATE] = after(gains, arrived[GAINS_GATE])
    gains = gather_gains(gains, chip)

    many = CHIPS * TOKENS
    own, table = pl.pallas_call(
        norm_kernel,
        out_shape=[
            shape(4, HEADS_PER_CHIP, many, HEAD_DIM),
            shape(many, HEAD_DIM, dtype=jnp.float32),
        ],
        in_specs=vmem(1 + CHIPS),
        out_specs=vmem(2),
        compiler_params=params(16),
        name="norm",
    )(gains, *arrived)
    other = swap(own)

    def attend(places, blocks):
        return pl.pallas_call(
            functools.partial(attend_kernel, places),
            out_shape=[shape(2 * BLOCK, HEAD_DIM)] * len(places),
            in_specs=vmem(4 + len(places)),
            out_specs=vmem(len(places)),
            compiler_params=params(32),
            name="attend",
        )(gains, table, own, other, *blocks)

    outs = dict(zip(EARLY, attend(EARLY, [arrived[place] for place in EARLY])))
    outs.update(zip(LATE, attend(LATE, late)))
    back = dict(zip(ORDER, send([outs[place] for place in ORDER], ORDER)))

    rows, width = q.shape
    attended, attended_tangent = pl.pallas_call(
        unpack_kernel,
        out_shape=[shape(rows, width)] * 2,
        in_specs=smem() + vmem(CHIPS),
        out_specs=vmem(2),
        compiler_params=params(16),
        name="unpack",
    )(chip_ref, *[back[place] for place in ORDER])
    return attended[None], attended_tangent[None]


def solution(mesh):
    rows = P("dp", "ctx", None)
    return jax.shard_map(
        local,
        mesh=mesh,
        in_specs=(rows,) * 6 + (P("dp"), P("dp")),
        out_specs=(rows, rows),
        check_vma=False,
    )
```
